512 devices in a mesh: dp: 32 (over z, y_hi), segment: 2 (over y_lo), mp: 8 (over x, core).
Axes of the slice: x: 4, y: 8 (y_hi: 4, y_lo: 2; y = y_hi * 2 + y_lo), z: 8, core: 2. Of those that a mesh axis runs over, the one named last changes fastest.
Arguments:
- prefix_hidden: bfloat16 [64, 512, 8192], P(('dp', 'segment'), 'mp'), may hold values from -16 to 16
- norm_gain: float32 [8192], replicated, may hold values from 0.5 to 1.5
- kv_weight: bfloat16 [8192, 2, 1024], P('dp', None, 'mp'), may hold values from -0.0625 to 0.0625
- action_query: bfloat16 [64, 128, 2048], P(('dp', 'segment'), None, 'mp'), may hold values from -104 to 104
- action_kv: bfloat16 [64, 128, 2, 1024], P(('dp', 'segment'), None, None, 'mp'), may hold values from -4.25 to 4.25
- out_cotangent: bfloat16 [64, 128, 2048], P(('dp', 'segment'), None, 'mp'), may hold values from -18 to 18
- prefix_blocks: int32 [64, 512], P(('dp', 'segment')), may hold values from 0 to 7, as said below
- action_blocks: int32 [64, 128], P(('dp', 'segment')), may hold values from 0 to 8, as said below
- prefix_lengths: int32 [64], P(('dp', 'segment')), may hold values from 128 to 512, as said below
- timesteps: int32 [64], P(('dp', 'segment')), may hold values from 0 to 999
Outputs:
- attn_out: bfloat16 [64, 128, 2048], P(('dp', 'segment'), None, 'mp')
- query_grad: float32 [64, 128, 2048], P(('dp', 'segment'), None, 'mp')
- action_kv_grad: float32 [64, 128, 2, 1024], P(('dp', 'segment'), None, None, 'mp')
- weight_grad: float32 [8192, 2, 1024], P('dp', None, 'mp')
The draws below stay inside these ranges and needn't reach their ends.
Inputs may be any that keep to these rules, and one draw needn't show every extreme that they name: `prefix_blocks`: constant over each run of 64 positions, 0 on the first run, rising by 0 or 1 from one run to the next; in every draw some sample rises at every run. `action_blocks`: constant over each run of 64 positions; the last run of every sample holds 8; in every draw some sample's first run holds 0. `prefix_lengths`: in every draw some sample's prefix is whole and some sample's is 128.
All inputs are finite; a program needn't handle non-finite values.
Results may differ from the reference program's by a relative error of at most 0.017.
Values may be sent and summed in bfloat16 or wider, within the bound.
No kernel may reach another device: no remote copies, remote signals or barrier semaphores. Data moves between devices by JAX's collectives and lax.ppermute only.
A program may use at most 64 MiB of HBM per device.

```python
import jax
import jax.numpy as jnp
from jax import lax

D = 8192
KVH = 8
HD = 128
QH = 16
PREFIX = 512
ACT = 128
TILE = 64
STEPS = 1000
SAMPLES = 64


def paired_actions(key):
    base = jax.random.fold_in(key, 31)
    pairs = jnp.clip(jax.random.normal(jax.random.fold_in(base, 1), (SAMPLES, ACT, 2, KVH * HD), jnp.float32), -4.0, 4.0)
    queries = jnp.clip(jax.random.normal(jax.random.fold_in(base, 2), (SAMPLES, ACT, QH * HD), jnp.float32), -4.0, 4.0)
    return (pairs, queries)


def draw_action_kv(key, part):
    return paired_actions(key)[0].astype(jnp.bfloat16)


def draw_action_query(key, part):
    return paired_actions(key)[1].astype(jnp.bfloat16)


def draw_prefix_blocks(key, part):
    tiles = PREFIX // TILE
    rises = jax.random.randint(jax.random.fold_in(key, 21), (SAMPLES, tiles), 0, 2)
    chosen = jax.random.randint(jax.random.fold_in(key, 25), (), 0, SAMPLES)
    rises = jnp.where((jnp.arange(SAMPLES) == chosen)[:, None], 1, rises)
    rises = rises.at[:, 0].set(0)
    levels = jnp.cumsum(rises, axis=1).astype(jnp.int32)
    return jnp.repeat(levels, TILE, axis=1).astype(jnp.int32)


def draw_action_blocks(key, part):
    tiles = ACT // TILE
    highest = PREFIX // TILE
    levels = jax.random.randint(jax.random.fold_in(key, 22), (SAMPLES, tiles), 0, highest + 1)
    chosen = jax.random.randint(jax.random.fold_in(key, 26), (), 0, SAMPLES)
    levels = levels.at[chosen, 0].set(0)
    levels = levels.at[:, tiles - 1].set(highest)
    return jnp.repeat(levels, TILE, axis=1).astype(jnp.int32)


def draw_prefix_lengths(key, part):
    lengths = jax.random.randint(jax.random.fold_in(key, 23), (SAMPLES,), PREFIX // 4, PREFIX + 1)
    chosen = jax.random.randint(jax.random.fold_in(key, 24), (), 0, SAMPLES)
    index = jnp.arange(SAMPLES)
    lengths = jnp.where(index == (chosen + 1) % SAMPLES, PREFIX // 4, lengths)
    return jnp.where(index == chosen, PREFIX, lengths).astype(jnp.int32)


def place_ends(entries, rng, smallest, largest):
    longest = entries.shape.index(max(entries.shape))
    spots = []
    for shift in (0, 1):
        where = [jax.random.randint(jax.random.fold_in(rng, axis), (), 0, length) for axis, length in enumerate(entries.shape)]
        where[longest] = (where[longest] + shift) % entries.shape[longest]
        spots.append(tuple(where))
    return entries.at[spots[0]].set(smallest).at[spots[1]].set(largest)


def spiked(result, stream_key, source, target, parts, factor):
    def block_of(axis_at):
        return (jnp.arange(result.shape[axis_at]) // (result.shape[axis_at] // parts)).reshape((-1,) + (1,) * (result.ndim - 1 - axis_at))

    near = jax.random.permutation(stream_key, parts)[block_of(target)]
    other_side = (block_of(target) + parts // 2) % parts
    return jnp.where((block_of(source) == near) | (block_of(source) == other_side), factor * result, result)


def shard_levels(own_key, extent, shards, least, largest):
    factor_of = 1.0
    for position, parts in shards:
        heights = jax.random.uniform(jax.random.fold_in(jax.random.fold_in(own_key, 6), position), (parts,), jnp.float32, least / len(shards), largest / len(shards))
        factor_of = factor_of * jnp.repeat(jnp.exp(heights), extent[position] // parts).reshape((-1,) + (1,) * (len(extent) - 1 - position))
    return factor_of


def centred(rng, extent, deviation, most, cuts=(), held_as=jnp.bfloat16):
    entries = deviation * jax.random.normal(rng, extent, jnp.float32)
    if cuts:
        entries = entries * shard_levels(rng, extent, cuts, -0.22, 0.18)
    return jnp.clip(entries, -most, most).astype(held_as)


def heavy_noise(key, shape, scale, limit, shards, heavy, kind=jnp.bfloat16):
    values = scale * jax.random.normal(key, shape, jnp.float32)
    if shards:
        values = values * shard_levels(key, shape, shards, -0.22, 0.18)
    return jnp.clip(spiked(values, jax.random.fold_in(key, 3), *heavy), -limit, limit).astype(kind)


def setup_inputs(seed: int = 0) -> dict:
    key_list = jax.random.split(jax.random.key(seed), 11)
    prefix_hidden = heavy_noise(key_list[0], (SAMPLES, PREFIX, D), 1.0, 16.0, ((0, 64), (1, 8)), (0, 2, 64, 4.0))
    norm_gain = jnp.clip(1.0 + 0.1 * jax.random.normal(key_list[1], (D,), jnp.float32), 0.5, 1.5)
    kv_weight = centred(key_list[2], (D, 2, KVH * HD), D ** -0.5, 0.0625, ((0, 32), (2, 8)))
    action_query = draw_action_query(jax.random.fold_in(key_list[10], 71), 0)
    action_kv = draw_action_kv(jax.random.fold_in(key_list[10], 71), 0)
    out_cotangent = centred(key_list[5], (SAMPLES, ACT, QH * HD), 3.0, 18.0, ((0, 64), (2, 8)))
    prefix_blocks = draw_prefix_blocks(jax.random.fold_in(key_list[10], 71), 0)
    action_blocks = draw_action_blocks(jax.random.fold_in(key_list[10], 71), 0)
    prefix_lengths = draw_prefix_lengths(jax.random.fold_in(key_list[10], 71), 0)
    timesteps = place_ends(jax.random.randint(key_list[9], (SAMPLES,), 0, STEPS), jax.random.fold_in(key_list[9], 1), 0, STEPS - 1).astype(jnp.int32)
    return dict(prefix_hidden=prefix_hidden, norm_gain=norm_gain, kv_weight=kv_weight, action_query=action_query, action_kv=action_kv, out_cotangent=out_cotangent, prefix_blocks=prefix_blocks, action_blocks=action_blocks, prefix_lengths=prefix_lengths, timesteps=timesteps)


EPS = 1e-06
NEGATIVE = -1e+30

def attention_pass(query, keys, values, visible, grad_out):
    scale = HD ** (-0.5)
    scores = jnp.einsum('agrh,jgh->graj', query.astype(jnp.float32), keys.astype(jnp.float32)) * scale
    masked = jnp.where(visible, scores, NEGATIVE)
    top = lax.optimization_barrier(jnp.max(masked, axis=-1, keepdims=True))
    expo = jnp.where(visible, jnp.exp(masked - top), 0.0)
    probs = expo / lax.optimization_barrier(jnp.sum(expo, axis=-1, keepdims=True))
    probs_low = lax.optimization_barrier(probs.astype(jnp.bfloat16)).astype(jnp.float32)
    out = jnp.einsum('graj,jgh->agrh', probs_low, values.astype(jnp.float32))
    d_probs = jnp.einsum('agrh,jgh->graj', grad_out.astype(jnp.float32), values.astype(jnp.float32))
    delta = lax.optimization_barrier(jnp.sum(probs * d_probs, axis=-1, keepdims=True))
    d_scores = lax.optimization_barrier((probs * (d_probs - delta)).astype(jnp.bfloat16)).astype(jnp.float32)
    d_query = jnp.einsum('graj,jgh->agrh', d_scores, keys.astype(jnp.float32)) * scale
    d_keys = jnp.einsum('graj,agrh->jgh', d_scores, query.astype(jnp.float32)) * scale
    d_values = jnp.einsum('graj,agrh->jgh', probs_low, grad_out.astype(jnp.float32))
    return (out, d_query, d_keys, d_values)

def reference(prefix_hidden, norm_gain, kv_weight, action_query, action_kv, out_cotangent, prefix_blocks, action_blocks, prefix_lengths, timesteps):
    ratio = QH // KVH
    columns = 2 * KVH * HD
    weight_flat = kv_weight.reshape(D, columns)
    positions = jnp.arange(PREFIX, dtype=jnp.int32)

    def one_sample(carry, inputs):
        hidden, query, own_pair, cotangent, pblocks, ablocks, length, level = inputs
        wide = hidden.astype(jnp.float32)
        inverse = lax.rsqrt(lax.optimization_barrier(jnp.mean(wide * wide, axis=-1, keepdims=True)) + EPS)
        normed = (wide * inverse * norm_gain).astype(jnp.bfloat16)
        prefix_kv = jnp.dot(normed, weight_flat, preferred_element_type=jnp.float32).astype(jnp.bfloat16)
        prefix_kv = prefix_kv.reshape(PREFIX, 2, KVH, HD)
        action_pair = own_pair.reshape(ACT, 2, KVH, HD)
        keys = jnp.concatenate([prefix_kv[:, 0], action_pair[:, 0]], axis=0)
        values = jnp.concatenate([prefix_kv[:, 1], action_pair[:, 1]], axis=0)
        see_prefix = (pblocks[None, :] <= ablocks[:, None]) & (positions[None, :] < length)
        see_action = ablocks[None, :] <= ablocks[:, None]
        visible = jnp.concatenate([see_prefix, see_action], axis=1)
        flow_weight = 0.5 + (level.astype(jnp.float32) + 0.5) / STEPS
        grad_out = (flow_weight * cotangent.astype(jnp.float32)).astype(jnp.bfloat16).reshape(ACT, KVH, ratio, HD)
        out, d_query, d_keys, d_values = attention_pass(query.reshape(ACT, KVH, ratio, HD), keys, values, visible, grad_out)
        d_pair = jnp.stack([d_keys, d_values], axis=1)
        prefix_grad = d_pair[:PREFIX].astype(jnp.bfloat16).reshape(PREFIX, columns)
        term = jnp.dot(normed.T, prefix_grad, preferred_element_type=jnp.float32)
        carry = carry + lax.optimization_barrier(term.astype(jnp.bfloat16)).astype(jnp.float32)
        results = (out.astype(jnp.bfloat16).reshape(ACT, QH * HD), d_query.reshape(ACT, QH * HD), d_pair[PREFIX:].reshape(ACT, 2, KVH * HD))
        return (carry, results)
    start = jnp.zeros((D, columns), jnp.float32)
    total, outputs = lax.scan(one_sample, start, (prefix_hidden, action_query, action_kv, out_cotangent, prefix_blocks, action_blocks, prefix_lengths, timesteps))
    attn_out, query_grad, action_kv_grad = outputs
    return (attn_out, query_grad, action_kv_grad, total.reshape(D, 2, KVH * HD))
```

```python
import jax
import jax.numpy as jnp
from jax import lax
from jax.sharding import Mesh
from jax.sharding import PartitionSpec as P

KVH = 8
HD = 128
QH = 16
STEPS = 1000
DP = ("dp_0", "dp_1")
EVERY = ("dp_0", "dp_1", "segment", "mp")
RING = 8
DP_SEGMENT = ("dp_0", "dp_1", "segment")


EPS = 1e-06
NEGATIVE = -1e30


def rings(along_z_core):
    groups = []
    for x in range(4):
        for core in range(2):
            for other in range(RING):
                places = [
                    (k, other) if core == along_z_core else (other, k) for k in range(RING)
                ]
                groups.append([((z * RING + y) * 4 + x) * 2 + core for z, y in places])
    return groups


FIRST = rings(0)
SECOND = rings(1)


def exchange(parts, groups):
    return lax.all_to_all(
        parts, EVERY, split_axis=0, concat_axis=0, tiled=True, axis_index_groups=groups
    )


def from_ring(array, groups):
    return exchange(jnp.broadcast_to(array, (RING, *array.shape)), groups)


def head_scores(query, keys):
    return jnp.einsum("agrh,jgh->graj", query, keys, preferred_element_type=jnp.float32) * HD ** (
        -0.5
    )


def backward_terms(probs, values, keys, query, grad_out):
    probs_low = probs.astype(jnp.bfloat16)
    d_probs = jnp.einsum("agrh,jgh->graj", grad_out, values, preferred_element_type=jnp.float32)
    delta = jnp.sum(probs * d_probs, axis=-1, keepdims=True)
    d_scores = (probs * (d_probs - delta)).astype(jnp.bfloat16)
    d_query = jnp.einsum(
        "graj,jgh->agrh", d_scores, keys, preferred_element_type=jnp.float32
    ) * HD ** (-0.5)
    d_keys = jnp.einsum(
        "graj,agrh->jgh", d_scores, query, preferred_element_type=jnp.float32
    ) * HD ** (-0.5)
    d_values = jnp.einsum("graj,agrh->jgh", probs_low, grad_out, preferred_element_type=jnp.float32)
    return (d_query, jnp.stack([d_keys, d_values], axis=1))


def shards(
    prefix_hidden,
    norm_gain,
    kv_weight,
    action_query,
    action_kv,
    out_cotangent,
    prefix_blocks,
    action_blocks,
    prefix_lengths,
    timesteps,
):
    acts = action_query.shape[1]
    heads_kv = kv_weight.shape[2] // HD
    ratio = QH // KVH
    columns = 2 * kv_weight.shape[2]
    wide = prefix_hidden[0].astype(jnp.float32)
    inverse = lax.rsqrt(jnp.mean(wide * wide, axis=-1, keepdims=True) + EPS)
    normed_local = (wide * inverse * norm_gain).astype(jnp.bfloat16)
    side = lax.axis_index("segment")
    core = lax.axis_index("mp") % 2
    local = kv_weight.reshape(kv_weight.shape[0], columns)
    normed_local, local = lax.optimization_barrier((normed_local, local))
    normed = lax.all_gather(normed_local, "mp", axis=0, tiled=True)
    rows = normed.shape[0]
    part = local.shape[0] // 2
    local = lax.dynamic_slice_in_dim(local, side * part, part, axis=0)
    plane = from_ring(from_ring(local, FIRST), SECOND)
    piece = jnp.where(core == 0, plane.swapaxes(0, 1), plane).reshape(RING * RING * part, columns)
    section = normed
    projected = jnp.dot(
        section, piece, preferred_element_type=jnp.float32
    )
    prefix_kv = projected.astype(jnp.bfloat16).reshape(rows, 2, heads_kv, HD)
    own_pair = action_kv[0].reshape(acts, 2, heads_kv, HD)
    query = action_query[0].reshape(acts, heads_kv, ratio, HD)
    flow_weight = 0.5 + (timesteps[0].astype(jnp.float32) + 0.5) / STEPS
    grad_out = (
        (flow_weight * out_cotangent[0].astype(jnp.float32))
        .astype(jnp.bfloat16)
        .reshape(acts, heads_kv, ratio, HD)
    )
    pblocks = prefix_blocks[0]
    ablocks = action_blocks[0]
    length = prefix_lengths[0]
    keys = jnp.concatenate([prefix_kv[:, 0], own_pair[:, 0]], axis=0)
    values = jnp.concatenate([prefix_kv[:, 1], own_pair[:, 1]], axis=0)
    positions = jnp.arange(rows, dtype=jnp.int32)
    see_prefix = (pblocks[None, :] <= ablocks[:, None]) & (positions[None, :] < length)
    see_action = ablocks[None, :] <= ablocks[:, None]
    visible = jnp.concatenate([see_prefix, see_action], axis=1)
    masked = jnp.where(visible, head_scores(query, keys), NEGATIVE)
    top = jnp.max(masked, axis=-1, keepdims=True)
    expo = jnp.where(visible, jnp.exp(masked - top), 0.0)
    probs = expo / jnp.sum(expo, axis=-1, keepdims=True)
    out = jnp.einsum(
        "graj,jgh->agrh", probs.astype(jnp.bfloat16), values, preferred_element_type=jnp.float32
    )
    d_query, d_pair = backward_terms(probs, values, keys, query, grad_out)
    d_prefix = d_pair[:rows]
    d_action = d_pair[rows:]
    attn_out = out.astype(jnp.bfloat16).reshape(1, acts, ratio * heads_kv * HD)
    query_grad = d_query.reshape(1, acts, ratio * heads_kv * HD)
    action_kv_grad = d_action.reshape(1, acts, 2, heads_kv * HD)
    prefix_grad = d_prefix.astype(jnp.bfloat16).reshape(rows, columns)
    section = normed
    term = lax.dot_general(
        section, prefix_grad, (((0,), (0,)), ((), ())), preferred_element_type=jnp.float32
    )
    term = term.astype(jnp.bfloat16).reshape(RING, RING, part, columns)
    term = jnp.where(core == 0, term.swapaxes(0, 1), term).reshape(RING * RING * part, columns)
    ring_sum = lax.psum_scatter(
        term, EVERY, scatter_dimension=0, tiled=True, axis_index_groups=SECOND
    )
    terms = exchange(ring_sum.reshape(RING, part, columns), FIRST)
    own = jnp.sum(terms.astype(jnp.float32), axis=0).astype(jnp.bfloat16)
    theirs = lax.ppermute(own, "segment", [(0, 1), (1, 0)])
    low = jnp.where(side == 0, own, theirs)
    high = jnp.where(side == 0, theirs, own)
    weight_grad = jnp.concatenate([low, high], axis=0).astype(jnp.float32)
    weight_grad = weight_grad.reshape(kv_weight.shape)
    return (attn_out, query_grad, action_kv_grad, weight_grad)


def solution(mesh):
    torus = Mesh(
        mesh.devices.reshape(8, 4, mesh.shape["segment"], mesh.shape["mp"]),
        ("dp_0", "dp_1", "segment", "mp"),
    )
    placed = (
        P(DP_SEGMENT, "mp", None),
        P(),
        P(DP, None, "mp"),
        P(DP_SEGMENT, None, "mp"),
        P(DP_SEGMENT, None, None, "mp"),
        P(DP_SEGMENT, None, "mp"),
        P(DP_SEGMENT, None),
        P(DP_SEGMENT, None),
        P(DP_SEGMENT),
        P(DP_SEGMENT),
    )
    return jax.shard_map(
        shards,
        mesh=torus,
        in_specs=placed,
        out_specs=(
            P(DP_SEGMENT, None, "mp"),
            P(DP_SEGMENT, None, "mp"),
            P(DP_SEGMENT, None, None, "mp"),
            P(DP, None, "mp"),
        ),
        check_vma=False,
    )
```

```python
import jax
import jax.numpy as jnp
from jax import lax
from jax.experimental import pallas as pl
from jax.experimental.pallas import tpu as pltpu
from jax.sharding import Mesh
from jax.sharding import PartitionSpec as P

D = 8192
KVH = 8
HD = 128
QH = 16
STEPS = 1000
PREFIX = 512
ACT = 128
DP = ("dp_0", "dp_1")
DP_SEGMENT = ("dp_0", "dp_1", "segment")
EVERY = ("dp_0", "dp_1", "segment", "mp")
RING = 8
PART = D // RING // RING
COLUMNS = 2 * HD
WIDE = D // RING


EPS = 1e-06
NEGATIVE = -1e30
UNSEEN = 1 << 20


def rings(along_z_core):
    groups = []
    for x in range(4):
        for core in range(2):
            for other in range(RING):
                places = [
                    (k, other) if core == along_z_core else (other, k) for k in range(RING)
                ]
                groups.append([((z * RING + y) * 4 + x) * 2 + core for z, y in places])
    return groups


FIRST = rings(0)
SECOND = rings(1)


def exchange(parts, groups):
    return lax.all_to_all(
        parts, EVERY, split_axis=0, concat_axis=0, tiled=True, axis_index_groups=groups
    )


def shifted(array, groups, offset):
    pairs = [
        (group[k], group[(k + offset) % RING]) for group in groups for k in range(RING)
    ]
    return lax.ppermute(array, EVERY, pairs)


def around(array, groups):
    half = array.shape[0] // 2
    behind2 = shifted(array, groups, 2)
    ahead2 = shifted(array, groups, -2)
    behind1 = shifted(array, groups, 1)
    ahead1 = shifted(array, groups, -1)
    behind3 = shifted(behind2, groups, 1)
    ahead3 = shifted(ahead2, groups, -1)
    opposite_low = shifted(behind2[:half], groups, 2)
    opposite_high = shifted(ahead2[half:], groups, -2)
    return (
        array,
        ahead1,
        ahead2,
        ahead3,
        opposite_low,
        opposite_high,
        behind3,
        behind2,
        behind1,
    )


def dot(a, b):
    return jnp.dot(a, b, preferred_element_type=jnp.float32)


def dot_t(a, b):
    return lax.dot_general(a, b, (((1,), (1,)), ((), ())), preferred_element_type=jnp.float32)


def flipped(a):
    return jnp.transpose(a.astype(jnp.float32))


def attend_kernel(
    normed_ref,
    w0,
    w1,
    w2,
    w3,
    w4l,
    w4h,
    w5,
    w6,
    w7,
    query_ref,
    pair_ref,
    cot_ref,
    levels_ref,
    alevels_ref,
    flow_ref,
    out_ref,
    dq_ref,
    dpair_ref,
    term_ref,
    x_buf,
    w_buf,
    t_buf,
    acc,
    x_sem,
    w_sem,
    t_sem,
):
    core = lax.rem(lax.axis_index("mp"), 2)
    place_z = lax.axis_index("dp_0")
    place_y = lax.axis_index("dp_1") * 2 + lax.axis_index("segment")
    me = jnp.where(core == 0, place_y, place_z)
    half = RING // 2
    pieces = [
        (w0, 0, 0, RING),
        (w1, 1, 0, RING),
        (w2, 2, 0, RING),
        (w3, 3, 0, RING),
        (w4l, 4, 0, half),
        (w4h, 4, half, half),
        (w5, 5, 0, RING),
        (w6, 6, 0, RING),
        (w7, 7, 0, RING),
    ]

    def x_copy(j):
        block = pl.ds(j * WIDE, WIDE)
        return pltpu.make_async_copy(normed_ref.at[:, block], x_buf.at[:, block], x_sem.at[j])

    for k, (ref, ahead, start, size) in enumerate(pieces):
        spot = lax.rem(me + ahead, RING)

        @pl.when(core == 0)
        def _():
            pltpu.make_async_copy(
                ref, w_buf.at[pl.ds(start, size), spot], w_sem.at[k]
            ).start()

        @pl.when(core == 1)
        def _():
            pltpu.make_async_copy(
                ref, w_buf.at[spot, pl.ds(start, size)], w_sem.at[k]
            ).start()

    for j in range(RING):
        x_copy(j).start()
    for k, (ref, ahead, start, size) in enumerate(pieces):
        pltpu.make_async_copy(ref, w_buf.at[0, pl.ds(start, size)], w_sem.at[k]).wait()
    for j in range(RING):
        x_copy(j).wait()
        product = dot(x_buf[:, j * WIDE : (j + 1) * WIDE], w_buf[j].reshape(WIDE, COLUMNS))
        if j == 0:
            acc[...] = product
        else:
            acc[...] += product
    scale = HD ** (-0.5)
    keys = jnp.concatenate([acc[:, :HD].astype(jnp.bfloat16), pair_ref[:, :HD]], axis=0)
    values = jnp.concatenate([acc[:, HD:].astype(jnp.bfloat16), pair_ref[:, HD:]], axis=0)
    grads = (flow_ref[0] * cot_ref[...].astype(jnp.float32)).astype(jnp.bfloat16)
    query = jnp.concatenate([query_ref[:, :HD], query_ref[:, HD:]], axis=0)
    grad_out = jnp.concatenate([grads[:, :HD], grads[:, HD:]], axis=0)
    alevels = jnp.concatenate([alevels_ref[...], alevels_ref[...]], axis=0)
    visible = levels_ref[...] <= alevels
    masked = jnp.where(visible, dot_t(query, keys) * scale, NEGATIVE)
    top = jnp.max(masked, axis=-1, keepdims=True)
    expo = jnp.where(visible, jnp.exp(masked - top), 0.0)
    probs = expo / jnp.sum(expo, axis=-1, keepdims=True)
    probs_low = probs.astype(jnp.bfloat16)
    d_probs = dot_t(grad_out, values)
    delta = jnp.sum(probs * d_probs, axis=-1, keepdims=True)
    d_scores = (probs * (d_probs - delta)).astype(jnp.bfloat16)
    query_t = jnp.concatenate([flipped(query[:ACT]), flipped(query[ACT:])], axis=1)
    grad_out_t = jnp.concatenate([flipped(grad_out[:ACT]), flipped(grad_out[ACT:])], axis=1)
    d_keys_t = dot(query_t.astype(jnp.bfloat16), d_scores) * scale
    d_values_t = dot(grad_out_t.astype(jnp.bfloat16), probs_low)
    prefix_t = jnp.concatenate([d_keys_t[:, :PREFIX], d_values_t[:, :PREFIX]], axis=0).astype(
        jnp.bfloat16
    )
    for j in range(RING):
        block = dot(prefix_t, x_buf[:, j * WIDE : (j + 1) * WIDE]).astype(jnp.bfloat16)
        for k in range(RING):
            t_buf[j, k] = block[:, k * PART : (k + 1) * PART]

        @pl.when(core == 0)
        def _():
            pltpu.make_async_copy(t_buf.at[j], term_ref.at[:, j], t_sem.at[j]).start()

        @pl.when(core == 1)
        def _():
            pltpu.make_async_copy(t_buf.at[j], term_ref.at[j], t_sem.at[j]).start()

    out = dot(probs_low, values)
    d_query = dot(d_scores, keys) * scale
    out_ref[:, :HD] = out[:ACT].astype(jnp.bfloat16)
    out_ref[:, HD:] = out[ACT:].astype(jnp.bfloat16)
    dq_ref[:, :HD] = d_query[:ACT]
    dq_ref[:, HD:] = d_query[ACT:]
    dpair_ref[:, :HD] = flipped(d_keys_t[:, PREFIX:])
    dpair_ref[:, HD:] = flipped(d_values_t[:, PREFIX:])
    for j in range(RING):
        pltpu.make_async_copy(t_buf.at[j], term_ref.at[j], t_sem.at[j]).wait()


def attend(normed, weights, query, pair, cotangent, levels, alevels, flow):
    vmem = pl.BlockSpec(memory_space=pltpu.VMEM)
    anywhere = pl.BlockSpec(memory_space=pl.ANY)
    smem = pl.BlockSpec(memory_space=pltpu.SMEM)
    return pl.pallas_call(
        attend_kernel,
        out_shape=(
            jax.ShapeDtypeStruct((ACT, COLUMNS), jnp.bfloat16),
            jax.ShapeDtypeStruct((ACT, COLUMNS), jnp.float32),
            jax.ShapeDtypeStruct((ACT, COLUMNS), jnp.float32),
            jax.ShapeDtypeStruct((RING, RING, COLUMNS, PART), jnp.bfloat16),
        ),
        in_specs=[anywhere] * 10 + [vmem] * 5 + [smem],
        out_specs=(vmem, vmem, vmem, anywhere),
        scratch_shapes=[
            pltpu.VMEM((PREFIX, D), jnp.bfloat16),
            pltpu.VMEM((RING, RING, PART, COLUMNS), jnp.bfloat16),
            pltpu.VMEM((RING, RING, COLUMNS, PART), jnp.bfloat16),
            pltpu.VMEM((PREFIX, COLUMNS), jnp.float32),
            pltpu.SemaphoreType.DMA((RING,)),
            pltpu.SemaphoreType.DMA((9,)),
            pltpu.SemaphoreType.DMA((RING,)),
        ],
        compiler_params=pltpu.CompilerParams(vmem_limit_bytes=40 * 2**20),
        cost_estimate=pl.CostEstimate(
            flops=4 * PREFIX * D * COLUMNS, bytes_accessed=16 * 2**20, transcendentals=163840
        ),
    )(normed, *weights, query, pair, cotangent, levels, alevels, flow)


def shards(
    prefix_hidden,
    norm_gain,
    kv_weight,
    action_query,
    action_kv,
    out_cotangent,
    prefix_blocks,
    action_blocks,
    prefix_lengths,
    timesteps,
):
    wide = prefix_hidden[0].astype(jnp.float32)
    inverse = lax.rsqrt(jnp.mean(wide * wide, axis=-1, keepdims=True) + EPS)
    normed_local = (wide * inverse * norm_gain).astype(jnp.bfloat16)
    side = lax.axis_index("segment")
    local = kv_weight.reshape(2 * PART, COLUMNS)
    normed_local, local = lax.optimization_barrier((normed_local, local))
    normed = lax.all_gather(normed_local, "mp", axis=0, tiled=True)
    local = lax.dynamic_slice_in_dim(local, side * PART, PART, axis=0)
    line = exchange(jnp.broadcast_to(local, (RING, *local.shape)), FIRST)
    weights = around(line, SECOND)
    flow_weight = 0.5 + (timesteps.astype(jnp.float32) + 0.5) / STEPS
    positions = jnp.arange(PREFIX, dtype=jnp.int32)
    levels = jnp.where(positions[None, :] < prefix_lengths[0], prefix_blocks, UNSEEN)
    levels = jnp.concatenate([levels, action_blocks], axis=1)
    out, d_query, d_action, term = attend(
        normed,
        weights,
        action_query[0],
        action_kv[0].reshape(ACT, COLUMNS),
        out_cotangent[0],
        levels,
        action_blocks.reshape(ACT, 1),
        flow_weight,
    )
    ring_sum = lax.psum_scatter(
        term.reshape(RING * RING * COLUMNS, PART),
        EVERY,
        scatter_dimension=0,
        tiled=True,
        axis_index_groups=SECOND,
    )
    terms = exchange(ring_sum.reshape(RING, COLUMNS, PART), FIRST)
    own = jnp.sum(terms.astype(jnp.float32), axis=0).astype(jnp.bfloat16)
    theirs = lax.ppermute(own, "segment", [(0, 1), (1, 0)])
    low = jnp.where(side == 0, own, theirs)
    high = jnp.where(side == 0, theirs, own)
    weight_grad = jnp.concatenate([low, high], axis=1).astype(jnp.float32).T
    return (
        out[None],
        d_query[None],
        d_action.reshape(1, ACT, 2, HD),
        weight_grad.reshape(2 * PART, 2, HD),
    )


def solution(mesh):
    torus = Mesh(
        mesh.devices.reshape(8, 4, mesh.shape["segment"], mesh.shape["mp"]),
        ("dp_0", "dp_1", "segment", "mp"),
    )
    placed = (
        P(DP_SEGMENT, "mp", None),
        P(),
        P(DP, None, "mp"),
        P(DP_SEGMENT, None, "mp"),
        P(DP_SEGMENT, None, None, "mp"),
        P(DP_SEGMENT, None, "mp"),
        P(DP_SEGMENT, None),
        P(DP_SEGMENT, None),
        P(DP_SEGMENT),
        P(DP_SEGMENT),
    )
    return jax.shard_map(
        shards,
        mesh=torus,
        in_specs=placed,
        out_specs=(
            P(DP_SEGMENT, None, "mp"),
            P(DP_SEGMENT, None, "mp"),
            P(DP_SEGMENT, None, None, "mp"),
            P(DP, None, "mp"),
        ),
        check_vma=False,
    )
```

```python
import jax
import jax.numpy as jnp
from jax import lax
from jax.experimental import pallas as pl
from jax.experimental.pallas import tpu as pltpu
from jax.sharding import Mesh
from jax.sharding import PartitionSpec as P

D = 8192
KVH = 8
HD = 128
QH = 16
STEPS = 1000
PREFIX = 512
ACT = 128
DP = ("dp_0", "dp_1")
DP_SEGMENT = ("dp_0", "dp_1", "segment")
EVERY = ("dp_0", "dp_1", "segment", "mp")
RING = 8
PART = D // RING // RING
COLUMNS = 2 * HD
WIDE = D // RING
NORM_ROWS = 32


EPS = 1e-06
NEGATIVE = -1e30
UNSEEN = 1 << 20


def rings(along_z_core):
    groups = []
    for x in range(4):
        for core in range(2):
            for other in range(RING):
                places = [
                    (k, other) if core == along_z_core else (other, k) for k in range(RING)
                ]
                groups.append([((z * RING + y) * 4 + x) * 2 + core for z, y in places])
    return groups


FIRST = rings(0)
SECOND = rings(1)


def exchange(parts, groups):
    return lax.all_to_all(
        parts, EVERY, split_axis=0, concat_axis=0, tiled=True, axis_index_groups=groups
    )


def shifted(array, groups, offset):
    pairs = [
        (group[k], group[(k + offset) % RING]) for group in groups for k in range(RING)
    ]
    return lax.ppermute(array, EVERY, pairs)


def around(array, groups, place):
    behind2 = shifted(array, groups, 2)
    ahead2 = shifted(array, groups, -2)
    behind1 = shifted(array, groups, 1)
    ahead1 = shifted(array, groups, -1)
    behind3 = shifted(behind2, groups, 1)
    ahead3 = shifted(ahead2, groups, -1)
    even = place % 2 == 0
    onward = [
        (group[k], group[(k + (2 if k % 2 == 0 else -2)) % RING])
        for group in groups
        for k in range(RING)
    ]
    opposite = lax.ppermute(jnp.where(even, behind2, ahead2), EVERY, onward)
    return (array, ahead1, ahead2, ahead3, opposite, behind3, behind2, behind1)


def norm_kernel(hidden_ref, gain_ref, out_ref):
    wide = hidden_ref[0].astype(jnp.float32)
    inverse = lax.rsqrt(jnp.mean(wide * wide, axis=-1, keepdims=True) + EPS)
    out_ref[...] = (wide * inverse * gain_ref[...]).astype(jnp.bfloat16)


def norm(hidden, gain):
    tokens = hidden.shape[1]
    return pl.pallas_call(
        norm_kernel,
        grid=(tokens // NORM_ROWS,),
        out_shape=jax.ShapeDtypeStruct((tokens, D), jnp.bfloat16),
        in_specs=[
            pl.BlockSpec((1, NORM_ROWS, D), lambda i: (0, i, 0)),
            pl.BlockSpec((1, D), lambda i: (0, 0)),
        ],
        out_specs=pl.BlockSpec((NORM_ROWS, D), lambda i: (i, 0)),
        cost_estimate=pl.CostEstimate(
            flops=4 * tokens * D, bytes_accessed=4 * tokens * D, transcendentals=tokens
        ),
    )(hidden, gain)


def dot(a, b):
    return jnp.dot(a, b, preferred_element_type=jnp.float32)


def dot_t(a, b):
    return lax.dot_general(a, b, (((1,), (1,)), ((), ())), preferred_element_type=jnp.float32)


def flipped(a):
    return jnp.transpose(a.astype(jnp.float32))


def attend_kernel(
    normed_ref,
    w0,
    w1,
    w2,
    w3,
    w4,
    w5,
    w6,
    w7,
    rows_ref,
    pair_ref,
    levels_ref,
    alevels_ref,
    out_ref,
    dq_ref,
    dpair_ref,
    term_ref,
    x_buf,
    w_buf,
    t_buf,
    acc,
    x_sem,
    w_sem,
    t_sem,
):
    core = lax.rem(lax.axis_index("mp"), 2)
    place_z = lax.axis_index("dp_0")
    place_y = lax.axis_index("dp_1") * 2 + lax.axis_index("segment")
    me = jnp.where(core == 0, place_y, place_z)
    pieces = (w0, w1, w2, w3, w4, w5, w6, w7)

    def x_copy(j):
        block = pl.ds(j * WIDE, WIDE)
        return pltpu.make_async_copy(normed_ref.at[:, block], x_buf.at[:, block], x_sem.at[j])

    for ahead, piece in enumerate(pieces):
        spot = lax.rem(me + ahead, RING)

        @pl.when(core == 0)
        def _():
            pltpu.make_async_copy(piece, w_buf.at[:, spot], w_sem.at[ahead]).start()

        @pl.when(core == 1)
        def _():
            pltpu.make_async_copy(piece, w_buf.at[spot], w_sem.at[ahead]).start()

    for j in range(RING):
        x_copy(j).start()
    for ahead, piece in enumerate(pieces):
        pltpu.make_async_copy(piece, w_buf.at[0], w_sem.at[ahead]).wait()
    acc[...] = jnp.zeros_like(acc)

    @pl.loop(0, RING)
    def _(j):
        x_copy(j).wait()
        block = x_buf[:, pl.ds(pl.multiple_of(j * WIDE, WIDE), WIDE)]
        acc[...] += dot(block, w_buf[j].reshape(WIDE, COLUMNS))

    scale = HD ** (-0.5)
    keys = jnp.concatenate([acc[:, :HD].astype(jnp.bfloat16), pair_ref[:, :HD]], axis=0)
    values = jnp.concatenate([acc[:, HD:].astype(jnp.bfloat16), pair_ref[:, HD:]], axis=0)
    query = jnp.concatenate([rows_ref[0, :, :HD], rows_ref[0, :, HD:]], axis=0)
    grad_out = jnp.concatenate([rows_ref[1, :, :HD], rows_ref[1, :, HD:]], axis=0)
    alevels = jnp.concatenate([alevels_ref[...], alevels_ref[...]], axis=0)
    visible = levels_ref[...] <= alevels
    masked = jnp.where(visible, dot_t(query, keys) * scale, NEGATIVE)
    top = jnp.max(masked, axis=-1, keepdims=True)
    expo = jnp.where(visible, jnp.exp(masked - top), 0.0)
    probs = expo / jnp.sum(expo, axis=-1, keepdims=True)
    probs_low = probs.astype(jnp.bfloat16)
    d_probs = dot_t(grad_out, values)
    delta = jnp.sum(probs * d_probs, axis=-1, keepdims=True)
    d_scores = (probs * (d_probs - delta)).astype(jnp.bfloat16)
    query_t = jnp.concatenate([flipped(query[:ACT]), flipped(query[ACT:])], axis=1)
    grad_out_t = jnp.concatenate([flipped(grad_out[:ACT]), flipped(grad_out[ACT:])], axis=1)
    d_keys_t = dot(query_t.astype(jnp.bfloat16), d_scores) * scale
    d_values_t = dot(grad_out_t.astype(jnp.bfloat16), probs_low)
    prefix_t = jnp.concatenate([d_keys_t[:, :PREFIX], d_values_t[:, :PREFIX]], axis=0).astype(
        jnp.bfloat16
    )
    for j in range(RING):
        block = dot(prefix_t, x_buf[:, j * WIDE : (j + 1) * WIDE]).astype(jnp.bfloat16)
        for k in range(RING):
            t_buf[j, k] = block[:, k * PART : (k + 1) * PART]

        @pl.when(core == 0)
        def _():
            pltpu.make_async_copy(t_buf.at[j], term_ref.at[:, j], t_sem.at[j]).start()

        @pl.when(core == 1)
        def _():
            pltpu.make_async_copy(t_buf.at[j], term_ref.at[j], t_sem.at[j]).start()

    out = dot(probs_low, values)
    d_query = dot(d_scores, keys) * scale
    out_ref[:, :HD] = out[:ACT].astype(jnp.bfloat16)
    out_ref[:, HD:] = out[ACT:].astype(jnp.bfloat16)
    dq_ref[:, :HD] = d_query[:ACT]
    dq_ref[:, HD:] = d_query[ACT:]
    dpair_ref[:, :HD] = flipped(d_keys_t[:, PREFIX:])
    dpair_ref[:, HD:] = flipped(d_values_t[:, PREFIX:])
    for j in range(RING):
        pltpu.make_async_copy(t_buf.at[j], term_ref.at[j], t_sem.at[j]).wait()


def attend(normed, weights, rows, pair, levels, alevels):
    vmem = pl.BlockSpec(memory_space=pltpu.VMEM)
    anywhere = pl.BlockSpec(memory_space=pl.ANY)
    hbm = pl.BlockSpec(memory_space=pltpu.HBM)
    return pl.pallas_call(
        attend_kernel,
        out_shape=(
            jax.ShapeDtypeStruct((ACT, COLUMNS), jnp.bfloat16),
            jax.ShapeDtypeStruct((ACT, COLUMNS), jnp.float32),
            jax.ShapeDtypeStruct((ACT, COLUMNS), jnp.float32),
            jax.ShapeDtypeStruct((RING, RING, COLUMNS, PART), jnp.bfloat16),
        ),
        in_specs=[hbm] + [anywhere] * 8 + [vmem] * 4,
        out_specs=(vmem, vmem, vmem, hbm),
        scratch_shapes=[
            pltpu.VMEM((PREFIX, D), jnp.bfloat16),
            pltpu.VMEM((RING, RING, PART, COLUMNS), jnp.bfloat16),
            pltpu.VMEM((RING, RING, COLUMNS, PART), jnp.bfloat16),
            pltpu.VMEM((PREFIX, COLUMNS), jnp.float32),
            pltpu.SemaphoreType.DMA((RING,)),
            pltpu.SemaphoreType.DMA((RING,)),
            pltpu.SemaphoreType.DMA((RING,)),
        ],
        compiler_params=pltpu.CompilerParams(vmem_limit_bytes=48 * 2**20),
        cost_estimate=pl.CostEstimate(
            flops=4 * PREFIX * D * COLUMNS, bytes_accessed=16 * 2**20, transcendentals=163840
        ),
    )(normed, *weights, rows, pair, levels, alevels)


def shards(
    prefix_hidden,
    norm_gain,
    kv_weight,
    action_query,
    action_kv,
    out_cotangent,
    prefix_blocks,
    action_blocks,
    prefix_lengths,
    timesteps,
):
    normed_local = norm(prefix_hidden, norm_gain.reshape(1, D))
    side = lax.axis_index("segment")
    local = kv_weight.reshape(2 * PART, COLUMNS)
    normed_local, local = lax.optimization_barrier((normed_local, local))
    normed = lax.all_gather(normed_local, "mp", axis=0, tiled=True)
    local = lax.dynamic_slice_in_dim(local, side * PART, PART, axis=0)
    line = exchange(jnp.broadcast_to(local, (RING, *local.shape)), FIRST)
    core = lax.axis_index("mp") % 2
    place = jnp.where(core == 0, lax.axis_index("dp_1") * 2 + side, lax.axis_index("dp_0"))
    weights = around(line, SECOND, place)
    flow_weight = 0.5 + (timesteps[0].astype(jnp.float32) + 0.5) / STEPS
    grad_out = (flow_weight * out_cotangent[0].astype(jnp.float32)).astype(jnp.bfloat16)
    positions = jnp.arange(PREFIX, dtype=jnp.int32)
    levels = jnp.where(positions[None, :] < prefix_lengths[0], prefix_blocks, UNSEEN)
    levels = jnp.concatenate([levels, action_blocks], axis=1)
    out, d_query, d_action, term = attend(
        normed,
        weights,
        jnp.stack([action_query[0], grad_out]),
        action_kv[0].reshape(ACT, COLUMNS),
        levels,
        action_blocks.reshape(ACT, 1),
    )
    ring_sum = lax.psum_scatter(
        term.reshape(RING * RING * COLUMNS, PART),
        EVERY,
        scatter_dimension=0,
        tiled=True,
        axis_index_groups=SECOND,
    )
    terms = exchange(ring_sum.reshape(RING, COLUMNS, PART), FIRST)
    own = jnp.sum(terms.astype(jnp.float32), axis=0).astype(jnp.bfloat16)
    theirs = lax.ppermute(own, "segment", [(0, 1), (1, 0)])
    low = jnp.where(side == 0, own, theirs)
    high = jnp.where(side == 0, theirs, own)
    weight_grad = jnp.concatenate([low, high], axis=1).astype(jnp.float32).T
    return (
        out[None],
        d_query[None],
        d_action.reshape(1, ACT, 2, HD),
        weight_grad.reshape(2 * PART, 2, HD),
    )


def solution(mesh):
    torus = Mesh(
        mesh.devices.reshape(8, 4, mesh.shape["segment"], mesh.shape["mp"]),
        ("dp_0", "dp_1", "segment", "mp"),
    )
    placed = (
        P(DP_SEGMENT, "mp", None),
        P(),
        P(DP, None, "mp"),
        P(DP_SEGMENT, None, "mp"),
        P(DP_SEGMENT, None, None, "mp"),
        P(DP_SEGMENT, None, "mp"),
        P(DP_SEGMENT, None),
        P(DP_SEGMENT, None),
        P(DP_SEGMENT),
        P(DP_SEGMENT),
    )
    return jax.shard_map(
        shards,
        mesh=torus,
        in_specs=placed,
        out_specs=(
            P(DP_SEGMENT, None, "mp"),
            P(DP_SEGMENT, None, "mp"),
            P(DP_SEGMENT, None, None, "mp"),
            P(DP, None, "mp"),
        ),
        check_vma=False,
    )
```

```python
import jax
import jax.numpy as jnp
from jax import lax
from jax.experimental import pallas as pl
from jax.experimental.pallas import tpu as pltpu
from jax.sharding import Mesh
from jax.sharding import PartitionSpec as P

D = 8192
KVH = 8
HD = 128
QH = 16
STEPS = 1000
PREFIX = 512
ACT = 128
DP = ("dp_0", "dp_1")
DP_SEGMENT = ("dp_0", "dp_1", "segment")
EVERY = ("dp_0", "dp_1", "segment", "mp")
RING = 8
PART = D // RING // RING
COLUMNS = 2 * HD
WIDE = D // RING
NORM_ROWS = 32


EPS = 1e-06
NEGATIVE = -1e30
UNSEEN = 1 << 20


def rings(along_z_core):
    groups = []
    for x in range(4):
        for core in range(2):
            for other in range(RING):
                places = [
                    (k, other) if core == along_z_core else (other, k) for k in range(RING)
                ]
                groups.append([((z * RING + y) * 4 + x) * 2 + core for z, y in places])
    return groups


FIRST = rings(0)
SECOND = rings(1)


def exchange(parts, groups):
    return lax.all_to_all(
        parts, EVERY, split_axis=0, concat_axis=0, tiled=True, axis_index_groups=groups
    )


def shifted(array, groups, offset):
    pairs = [
        (group[k], group[(k + offset) % RING]) for group in groups for k in range(RING)
    ]
    return lax.ppermute(array, EVERY, pairs)


def around(array, groups, place):
    behind2 = shifted(array, groups, 2)
    ahead2 = shifted(array, groups, -2)
    behind1 = shifted(array, groups, 1)
    ahead1 = shifted(array, groups, -1)
    behind3 = shifted(behind2, groups, 1)
    ahead3 = shifted(ahead2, groups, -1)
    even = place % 2 == 0
    onward = [
        (group[k], group[(k + (2 if k % 2 == 0 else -2)) % RING])
        for group in groups
        for k in range(RING)
    ]
    opposite = lax.ppermute(jnp.where(even, behind2, ahead2), EVERY, onward)
    return (array, ahead1, ahead2, ahead3, opposite, behind3, behind2, behind1)


def norm_kernel(hidden_ref, gain_ref, out_ref):
    wide = hidden_ref[0].astype(jnp.float32)
    inverse = lax.rsqrt(jnp.mean(wide * wide, axis=-1, keepdims=True) + EPS)
    out_ref[...] = (wide * inverse * gain_ref[...]).astype(jnp.bfloat16)


def norm(hidden, gain):
    tokens = hidden.shape[1]
    return pl.pallas_call(
        norm_kernel,
        grid=(tokens // NORM_ROWS,),
        out_shape=jax.ShapeDtypeStruct((tokens, D), jnp.bfloat16),
        in_specs=[
            pl.BlockSpec((1, NORM_ROWS, D), lambda i: (0, i, 0)),
            pl.BlockSpec((1, D), lambda i: (0, 0)),
        ],
        out_specs=pl.BlockSpec((NORM_ROWS, D), lambda i: (i, 0)),
        cost_estimate=pl.CostEstimate(
            flops=4 * tokens * D, bytes_accessed=4 * tokens * D, transcendentals=tokens
        ),
    )(hidden, gain)


def dot(a, b):
    return jnp.dot(a, b, preferred_element_type=jnp.float32)


def dot_t(a, b):
    return lax.dot_general(a, b, (((1,), (1,)), ((), ())), preferred_element_type=jnp.float32)


def flipped(a):
    return jnp.transpose(a.astype(jnp.float32))


def attend_kernel(
    normed_ref,
    w0,
    w1,
    w2,
    w3,
    w4,
    w5,
    w6,
    w7,
    rows_ref,
    pair_ref,
    levels_ref,
    alevels_ref,
    out_ref,
    dq_ref,
    dpair_ref,
    term_ref,
    x_buf,
    w_buf,
    t_buf,
    acc,
    x_sem,
    w_sem,
    t_sem,
):
    core = lax.rem(lax.axis_index("mp"), 2)
    place_z = lax.axis_index("dp_0")
    place_y = lax.axis_index("dp_1") * 2 + lax.axis_index("segment")
    me = jnp.where(core == 0, place_y, place_z)
    pieces = (w0, w1, w2, w3, w4, w5, w6, w7)

    def x_copy(j):
        block = pl.ds(j * WIDE, WIDE)
        return pltpu.make_async_copy(normed_ref.at[:, block], x_buf.at[:, block], x_sem.at[j])

    for ahead, piece in enumerate(pieces):
        spot = lax.rem(me + ahead, RING)

        @pl.when(core == 0)
        def _():
            pltpu.make_async_copy(piece, w_buf.at[:, spot], w_sem.at[ahead]).start()

        @pl.when(core == 1)
        def _():
            pltpu.make_async_copy(piece, w_buf.at[spot], w_sem.at[ahead]).start()

    for j in range(RING):
        x_copy(j).start()
    for ahead, piece in enumerate(pieces):
        pltpu.make_async_copy(piece, w_buf.at[0], w_sem.at[ahead]).wait()
    acc[...] = jnp.zeros_like(acc)

    @pl.loop(0, RING)
    def _(j):
        x_copy(j).wait()
        block = x_buf[:, pl.ds(pl.multiple_of(j * WIDE, WIDE), WIDE)]
        acc[...] += dot(block, w_buf[j].reshape(WIDE, COLUMNS))

    scale = HD ** (-0.5)
    keys = jnp.concatenate([acc[:, :HD].astype(jnp.bfloat16), pair_ref[:, :HD]], axis=0)
    values = jnp.concatenate([acc[:, HD:].astype(jnp.bfloat16), pair_ref[:, HD:]], axis=0)
    query = jnp.concatenate([rows_ref[0, :, :HD], rows_ref[0, :, HD:]], axis=0)
    grad_out = jnp.concatenate([rows_ref[1, :, :HD], rows_ref[1, :, HD:]], axis=0)
    alevels = jnp.concatenate([alevels_ref[...], alevels_ref[...]], axis=0)
    visible = levels_ref[...] <= alevels
    masked = jnp.where(visible, dot_t(query, keys) * scale, NEGATIVE)
    top = jnp.max(masked, axis=-1, keepdims=True)
    expo = jnp.where(visible, jnp.exp(masked - top), 0.0)
    probs = expo / jnp.sum(expo, axis=-1, keepdims=True)
    probs_low = probs.astype(jnp.bfloat16)
    d_probs = dot_t(grad_out, values)
    delta = jnp.sum(probs * d_probs, axis=-1, keepdims=True)
    d_scores = (probs * (d_probs - delta)).astype(jnp.bfloat16)
    query_t = jnp.concatenate([flipped(query[:ACT]), flipped(query[ACT:])], axis=1)
    grad_out_t = jnp.concatenate([flipped(grad_out[:ACT]), flipped(grad_out[ACT:])], axis=1)
    d_keys_t = dot(query_t.astype(jnp.bfloat16), d_scores) * scale
    d_values_t = dot(grad_out_t.astype(jnp.bfloat16), probs_low)
    prefix_t = jnp.concatenate([d_keys_t[:, :PREFIX], d_values_t[:, :PREFIX]], axis=0).astype(
        jnp.bfloat16
    )
    for j in range(RING):
        block = dot(prefix_t, x_buf[:, j * WIDE : (j + 1) * WIDE]).astype(jnp.bfloat16)
        for k in range(RING):
            t_buf[j, k] = block[:, k * PART : (k + 1) * PART]

        @pl.when(core == 0)
        def _():
            pltpu.make_async_copy(t_buf.at[j], term_ref.at[:, j], t_sem.at[j]).start()

        @pl.when(core == 1)
        def _():
            pltpu.make_async_copy(t_buf.at[j], term_ref.at[j], t_sem.at[j]).start()

    out = dot(probs_low, values)
    d_query = dot(d_scores, keys) * scale
    out_ref[:, :HD] = out[:ACT].astype(jnp.bfloat16)
    out_ref[:, HD:] = out[ACT:].astype(jnp.bfloat16)
    dq_ref[:, :HD] = d_query[:ACT]
    dq_ref[:, HD:] = d_query[ACT:]
    dpair_ref[:, :HD] = flipped(d_keys_t[:, PREFIX:])
    dpair_ref[:, HD:] = flipped(d_values_t[:, PREFIX:])
    for j in range(RING):
        pltpu.make_async_copy(t_buf.at[j], term_ref.at[j], t_sem.at[j]).wait()


def attend(normed, weights, rows, pair, levels, alevels):
    vmem = pl.BlockSpec(memory_space=pltpu.VMEM)
    anywhere = pl.BlockSpec(memory_space=pl.ANY)
    hbm = pl.BlockSpec(memory_space=pltpu.HBM)
    return pl.pallas_call(
        attend_kernel,
        out_shape=(
            jax.ShapeDtypeStruct((ACT, COLUMNS), jnp.bfloat16),
            jax.ShapeDtypeStruct((ACT, COLUMNS), jnp.float32),
            jax.ShapeDtypeStruct((ACT, COLUMNS), jnp.float32),
            jax.ShapeDtypeStruct((RING, RING, COLUMNS, PART), jnp.bfloat16),
        ),
        in_specs=[hbm] + [anywhere] * 8 + [vmem] * 4,
        out_specs=(vmem, vmem, vmem, hbm),
        scratch_shapes=[
            pltpu.VMEM((PREFIX, D), jnp.bfloat16),
            pltpu.VMEM((RING, RING, PART, COLUMNS), jnp.bfloat16),
            pltpu.VMEM((RING, RING, COLUMNS, PART), jnp.bfloat16),
            pltpu.VMEM((PREFIX, COLUMNS), jnp.float32),
            pltpu.SemaphoreType.DMA((RING,)),
            pltpu.SemaphoreType.DMA((RING,)),
            pltpu.SemaphoreType.DMA((RING,)),
        ],
        compiler_params=pltpu.CompilerParams(vmem_limit_bytes=48 * 2**20),
        cost_estimate=pl.CostEstimate(
            flops=4 * PREFIX * D * COLUMNS, bytes_accessed=16 * 2**20, transcendentals=163840
        ),
    )(normed, *weights, rows, pair, levels, alevels)


def shards(
    prefix_hidden,
    norm_gain,
    kv_weight,
    action_query,
    action_kv,
    out_cotangent,
    prefix_blocks,
    action_blocks,
    prefix_lengths,
    timesteps,
):
    normed_local = norm(prefix_hidden, norm_gain.reshape(1, D))
    side = lax.axis_index("segment")
    normed_local, local = lax.optimization_barrier((normed_local, kv_weight))
    normed = lax.all_gather(normed_local, "mp", axis=0, tiled=True)
    local = lax.dynamic_slice_in_dim(local, side * PART, PART, axis=0).reshape(PART, COLUMNS)
    line = exchange(jnp.broadcast_to(local, (RING, *local.shape)), FIRST)
    core = lax.axis_index("mp") % 2
    place = jnp.where(core == 0, lax.axis_index("dp_1") * 2 + side, lax.axis_index("dp_0"))
    weights = around(line, SECOND, place)
    flow_weight = 0.5 + (timesteps[0].astype(jnp.float32) + 0.5) / STEPS
    grad_out = (flow_weight * out_cotangent[0].astype(jnp.float32)).astype(jnp.bfloat16)
    positions = jnp.arange(PREFIX, dtype=jnp.int32)
    levels = jnp.where(positions[None, :] < prefix_lengths[0], prefix_blocks, UNSEEN)
    levels = jnp.concatenate([levels, action_blocks], axis=1)
    out, d_query, d_action, term = attend(
        normed,
        weights,
        jnp.stack([action_query[0], grad_out]),
        action_kv[0].reshape(ACT, COLUMNS),
        levels,
        action_blocks.reshape(ACT, 1),
    )
    ring_sum = lax.psum_scatter(
        term.reshape(RING * RING * COLUMNS, PART),
        EVERY,
        scatter_dimension=0,
        tiled=True,
        axis_index_groups=SECOND,
    )
    terms = exchange(ring_sum.reshape(RING, COLUMNS, PART), FIRST)
    own = jnp.sum(terms.astype(jnp.float32), axis=0).astype(jnp.bfloat16)
    theirs = lax.ppermute(own, "segment", [(0, 1), (1, 0)])
    low = jnp.where(side == 0, own, theirs)
    high = jnp.where(side == 0, theirs, own)
    weight_grad = jnp.concatenate([low, high], axis=1).astype(jnp.float32).T
    return (
        out[None],
        d_query[None],
        d_action.reshape(1, ACT, 2, HD),
        weight_grad.reshape(2 * PART, 2, HD),
    )


def solution(mesh):
    torus = Mesh(
        mesh.devices.reshape(8, 4, mesh.shape["segment"], mesh.shape["mp"]),
        ("dp_0", "dp_1", "segment", "mp"),
    )
    placed = (
        P(DP_SEGMENT, "mp", None),
        P(),
        P(DP, None, "mp"),
        P(DP_SEGMENT, None, "mp"),
        P(DP_SEGMENT, None, None, "mp"),
        P(DP_SEGMENT, None, "mp"),
        P(DP_SEGMENT, None),
        P(DP_SEGMENT, None),
        P(DP_SEGMENT),
        P(DP_SEGMENT),
    )
    return jax.shard_map(
        shards,
        mesh=torus,
        in_specs=placed,
        out_specs=(
            P(DP_SEGMENT, None, "mp"),
            P(DP_SEGMENT, None, "mp"),
            P(DP_SEGMENT, None, None, "mp"),
            P(DP, None, "mp"),
        ),
        check_vma=False,
    )
```

```python
import jax
import jax.numpy as jnp
from jax import lax
from jax.experimental import pallas as pl
from jax.experimental.pallas import tpu as pltpu
from jax.sharding import Mesh
from jax.sharding import PartitionSpec as P

D = 8192
KVH = 8
HD = 128
QH = 16
STEPS = 1000
PREFIX = 512
ACT = 128
DP = ("dp_0", "dp_1")
DP_SEGMENT = ("dp_0", "dp_1", "segment")
EVERY = ("dp_0", "dp_1", "segment", "mp")
RING = 8
PART = D // RING // RING
COLUMNS = 2 * HD
WIDE = D // RING
NORM_ROWS = 32


EPS = 1e-06
NEGATIVE = -1e30
UNSEEN = 1 << 20


def rings(along_z_core):
    groups = []
    for x in range(4):
        for core in range(2):
            for other in range(RING):
                places = [
                    (k, other) if core == along_z_core else (other, k) for k in range(RING)
                ]
                groups.append([((z * RING + y) * 4 + x) * 2 + core for z, y in places])
    return groups


FIRST = rings(0)
SECOND = rings(1)


def exchange(parts, groups):
    return lax.all_to_all(
        parts, EVERY, split_axis=0, concat_axis=0, tiled=True, axis_index_groups=groups
    )


def shifted(array, groups, offset):
    pairs = [
        (group[k], group[(k + offset) % RING]) for group in groups for k in range(RING)
    ]
    return lax.ppermute(array, EVERY, pairs)


def around(array, groups, place, raw, prepare):
    behind2 = shifted(array, groups, 2)
    ahead2 = shifted(array, groups, -2)
    behind1 = shifted(array, groups, 1)
    ahead1 = shifted(array, groups, -1)
    behind2, raw = lax.optimization_barrier((behind2, raw))
    ahead2, others = lax.optimization_barrier((ahead2, prepare(*raw)))
    behind3 = shifted(behind2, groups, 1)
    ahead3 = shifted(ahead2, groups, -1)
    even = place % 2 == 0
    onward = [
        (group[k], group[(k + (2 if k % 2 == 0 else -2)) % RING])
        for group in groups
        for k in range(RING)
    ]
    opposite = lax.ppermute(jnp.where(even, behind2, ahead2), EVERY, onward)
    weights = (array, ahead1, ahead2, ahead3, opposite, behind3, behind2, behind1)
    return weights, others


def norm_kernel(hidden_ref, gain_ref, out_ref):
    wide = hidden_ref[0].astype(jnp.float32)
    inverse = lax.rsqrt(jnp.mean(wide * wide, axis=-1, keepdims=True) + EPS)
    out_ref[...] = (wide * inverse * gain_ref[...]).astype(jnp.bfloat16)


def norm(hidden, gain):
    tokens = hidden.shape[1]
    return pl.pallas_call(
        norm_kernel,
        grid=(tokens // NORM_ROWS,),
        out_shape=jax.ShapeDtypeStruct((tokens, D), jnp.bfloat16),
        in_specs=[
            pl.BlockSpec((1, NORM_ROWS, D), lambda i: (0, i, 0)),
            pl.BlockSpec((1, D), lambda i: (0, 0)),
        ],
        out_specs=pl.BlockSpec((NORM_ROWS, D), lambda i: (i, 0)),
        cost_estimate=pl.CostEstimate(
            flops=4 * tokens * D, bytes_accessed=4 * tokens * D, transcendentals=tokens
        ),
    )(hidden, gain)


def dot(a, b):
    return jnp.dot(a, b, preferred_element_type=jnp.float32)


def dot_t(a, b):
    return lax.dot_general(a, b, (((1,), (1,)), ((), ())), preferred_element_type=jnp.float32)


def flipped(a):
    return jnp.transpose(a.astype(jnp.float32))


def attend_kernel(
    normed_ref,
    w0,
    w1,
    w2,
    w3,
    w4,
    w5,
    w6,
    w7,
    rows_ref,
    pair_ref,
    levels_ref,
    alevels_ref,
    out_ref,
    dq_ref,
    dpair_ref,
    term_ref,
    x_buf,
    w_buf,
    t_buf,
    acc,
    x_sem,
    w_sem,
    t_sem,
):
    core = lax.rem(lax.axis_index("mp"), 2)
    place_z = lax.axis_index("dp_0")
    place_y = lax.axis_index("dp_1") * 2 + lax.axis_index("segment")
    me = jnp.where(core == 0, place_y, place_z)
    pieces = (w0, w1, w2, w3, w4, w5, w6, w7)

    def x_copy(j):
        block = pl.ds(j * WIDE, WIDE)
        return pltpu.make_async_copy(normed_ref.at[:, block], x_buf.at[:, block], x_sem.at[j])

    for ahead, piece in enumerate(pieces):
        spot = lax.rem(me + ahead, RING)

        @pl.when(core == 0)
        def _():
            pltpu.make_async_copy(piece, w_buf.at[:, spot], w_sem.at[ahead]).start()

        @pl.when(core == 1)
        def _():
            pltpu.make_async_copy(piece, w_buf.at[spot], w_sem.at[ahead]).start()

    for j in range(RING):
        x_copy(j).start()
    for ahead, piece in enumerate(pieces):
        pltpu.make_async_copy(piece, w_buf.at[0], w_sem.at[ahead]).wait()
    acc[...] = jnp.zeros_like(acc)

    @pl.loop(0, RING)
    def _(j):
        x_copy(j).wait()
        block = x_buf[:, pl.ds(pl.multiple_of(j * WIDE, WIDE), WIDE)]
        acc[...] += dot(block, w_buf[j].reshape(WIDE, COLUMNS))

    scale = HD ** (-0.5)
    keys = jnp.concatenate([acc[:, :HD].astype(jnp.bfloat16), pair_ref[:, :HD]], axis=0)
    values = jnp.concatenate([acc[:, HD:].astype(jnp.bfloat16), pair_ref[:, HD:]], axis=0)
    query = jnp.concatenate([rows_ref[0, :, :HD], rows_ref[0, :, HD:]], axis=0)
    grad_out = jnp.concatenate([rows_ref[1, :, :HD], rows_ref[1, :, HD:]], axis=0)
    alevels = jnp.concatenate([alevels_ref[...], alevels_ref[...]], axis=0)
    visible = levels_ref[...] <= alevels
    masked = jnp.where(visible, dot_t(query, keys) * scale, NEGATIVE)
    top = jnp.max(masked, axis=-1, keepdims=True)
    expo = jnp.where(visible, jnp.exp(masked - top), 0.0)
    probs = expo / jnp.sum(expo, axis=-1, keepdims=True)
    probs_low = probs.astype(jnp.bfloat16)
    d_probs = dot_t(grad_out, values)
    delta = jnp.sum(probs * d_probs, axis=-1, keepdims=True)
    d_scores = (probs * (d_probs - delta)).astype(jnp.bfloat16)
    query_t = jnp.concatenate([flipped(query[:ACT]), flipped(query[ACT:])], axis=1)
    grad_out_t = jnp.concatenate([flipped(grad_out[:ACT]), flipped(grad_out[ACT:])], axis=1)
    d_keys_t = dot(query_t.astype(jnp.bfloat16), d_scores) * scale
    d_values_t = dot(grad_out_t.astype(jnp.bfloat16), probs_low)
    prefix_t = jnp.concatenate([d_keys_t[:, :PREFIX], d_values_t[:, :PREFIX]], axis=0).astype(
        jnp.bfloat16
    )
    for j in range(RING):
        block = dot(prefix_t, x_buf[:, j * WIDE : (j + 1) * WIDE]).astype(jnp.bfloat16)
        for k in range(RING):
            t_buf[j, k] = block[:, k * PART : (k + 1) * PART]

        @pl.when(core == 0)
        def _():
            pltpu.make_async_copy(t_buf.at[j], term_ref.at[:, j], t_sem.at[j]).start()

        @pl.when(core == 1)
        def _():
            pltpu.make_async_copy(t_buf.at[j], term_ref.at[j], t_sem.at[j]).start()

    out = dot(probs_low, values)
    d_query = dot(d_scores, keys) * scale
    out_ref[:, :HD] = out[:ACT].astype(jnp.bfloat16)
    out_ref[:, HD:] = out[ACT:].astype(jnp.bfloat16)
    dq_ref[:, :HD] = d_query[:ACT]
    dq_ref[:, HD:] = d_query[ACT:]
    dpair_ref[:, :HD] = flipped(d_keys_t[:, PREFIX:])
    dpair_ref[:, HD:] = flipped(d_values_t[:, PREFIX:])
    for j in range(RING):
        pltpu.make_async_copy(t_buf.at[j], term_ref.at[j], t_sem.at[j]).wait()


def attend(normed, weights, rows, pair, levels, alevels):
    vmem = pl.BlockSpec(memory_space=pltpu.VMEM)
    anywhere = pl.BlockSpec(memory_space=pl.ANY)
    hbm = pl.BlockSpec(memory_space=pltpu.HBM)
    return pl.pallas_call(
        attend_kernel,
        out_shape=(
            jax.ShapeDtypeStruct((ACT, COLUMNS), jnp.bfloat16),
            jax.ShapeDtypeStruct((ACT, COLUMNS), jnp.float32),
            jax.ShapeDtypeStruct((ACT, COLUMNS), jnp.float32),
            jax.ShapeDtypeStruct((RING, RING, COLUMNS, PART), jnp.bfloat16),
        ),
        in_specs=[hbm] + [anywhere] * 8 + [vmem] * 4,
        out_specs=(vmem, vmem, vmem, hbm),
        scratch_shapes=[
            pltpu.VMEM((PREFIX, D), jnp.bfloat16),
            pltpu.VMEM((RING, RING, PART, COLUMNS), jnp.bfloat16),
            pltpu.VMEM((RING, RING, COLUMNS, PART), jnp.bfloat16),
            pltpu.VMEM((PREFIX, COLUMNS), jnp.float32),
            pltpu.SemaphoreType.DMA((RING,)),
            pltpu.SemaphoreType.DMA((RING,)),
            pltpu.SemaphoreType.DMA((RING,)),
        ],
        compiler_params=pltpu.CompilerParams(vmem_limit_bytes=48 * 2**20),
        cost_estimate=pl.CostEstimate(
            flops=4 * PREFIX * D * COLUMNS, bytes_accessed=16 * 2**20, transcendentals=163840
        ),
    )(normed, *weights, rows, pair, levels, alevels)


def prepare(query, pair, cotangent, prefix_blocks, action_blocks, prefix_lengths, timesteps):
    flow_weight = 0.5 + (timesteps[0].astype(jnp.float32) + 0.5) / STEPS
    grad_out = (flow_weight * cotangent[0].astype(jnp.float32)).astype(jnp.bfloat16)
    positions = jnp.arange(PREFIX, dtype=jnp.int32)
    levels = jnp.where(positions[None, :] < prefix_lengths[0], prefix_blocks, UNSEEN)
    return (
        jnp.stack([query[0], grad_out]),
        pair[0].reshape(ACT, COLUMNS),
        jnp.concatenate([levels, action_blocks], axis=1),
        action_blocks.reshape(ACT, 1),
    )


def shards(
    prefix_hidden,
    norm_gain,
    kv_weight,
    action_query,
    action_kv,
    out_cotangent,
    prefix_blocks,
    action_blocks,
    prefix_lengths,
    timesteps,
):
    normed_local = norm(prefix_hidden, norm_gain.reshape(1, D))
    side = lax.axis_index("segment")
    normed_local, local = lax.optimization_barrier((normed_local, kv_weight))
    normed = lax.all_gather(normed_local, "mp", axis=0, tiled=True)
    local = lax.dynamic_slice_in_dim(local, side * PART, PART, axis=0).reshape(PART, COLUMNS)
    line = exchange(jnp.broadcast_to(local, (RING, *local.shape)), FIRST)
    core = lax.axis_index("mp") % 2
    place = jnp.where(core == 0, lax.axis_index("dp_1") * 2 + side, lax.axis_index("dp_0"))
    raw = (
        action_query,
        action_kv,
        out_cotangent,
        prefix_blocks,
        action_blocks,
        prefix_lengths,
        timesteps,
    )
    weights, others = around(line, SECOND, place, raw, prepare)
    out, d_query, d_action, term = attend(normed, weights, *others)
    ring_sum = lax.psum_scatter(
        term.reshape(RING * RING * COLUMNS, PART),
        EVERY,
        scatter_dimension=0,
        tiled=True,
        axis_index_groups=SECOND,
    )
    terms = exchange(ring_sum.reshape(RING, COLUMNS, PART), FIRST)
    own = jnp.sum(terms.astype(jnp.float32), axis=0).astype(jnp.bfloat16)
    theirs = lax.ppermute(own, "segment", [(0, 1), (1, 0)])
    low = jnp.where(side == 0, own, theirs)
    high = jnp.where(side == 0, theirs, own)
    weight_grad = jnp.concatenate([low, high], axis=1).astype(jnp.float32).T
    return (
        out[None],
        d_query[None],
        d_action.reshape(1, ACT, 2, HD),
        weight_grad.reshape(2 * PART, 2, HD),
    )


def solution(mesh):
    torus = Mesh(
        mesh.devices.reshape(8, 4, mesh.shape["segment"], mesh.shape["mp"]),
        ("dp_0", "dp_1", "segment", "mp"),
    )
    placed = (
        P(DP_SEGMENT, "mp", None),
        P(),
        P(DP, None, "mp"),
        P(DP_SEGMENT, None, "mp"),
        P(DP_SEGMENT, None, None, "mp"),
        P(DP_SEGMENT, None, "mp"),
        P(DP_SEGMENT, None),
        P(DP_SEGMENT, None),
        P(DP_SEGMENT),
        P(DP_SEGMENT),
    )
    return jax.shard_map(
        shards,
        mesh=torus,
        in_specs=placed,
        out_specs=(
            P(DP_SEGMENT, None, "mp"),
            P(DP_SEGMENT, None, "mp"),
            P(DP_SEGMENT, None, None, "mp"),
            P(DP, None, "mp"),
        ),
        check_vma=False,
    )
```
